512 devices in a mesh: leaf: 512 (over y, x, z, core).
Axes of the slice: x: 4, y: 4, z: 16, core: 2. Of those that a mesh axis runs over, the one named last changes fastest.
Arguments:
- values: float32 [524288, 128], P('leaf'), may hold values from -6 to 6
- coords: float32 [3, 524288], P(None, 'leaf'), may hold values from 0 to 2.5, as said below
- permutation: int32 [524288], P('leaf'), may hold values from 0 to 524287, as said below
- basis: float32 [524288, 256], P('leaf'), may hold values from -0.1875 to 0.1875
- transfers: float32 [229376, 256], P('leaf'), may hold values from -0.375 to 0.375
- couplings: float32 [491520, 256], P('leaf'), may hold values from -0.375 to 0.375
- interactions: int32 [512, 4, 2], P('leaf'), may hold values from 0 to 511, as said below
Outputs:
- product: float32 [524288, 128], P('leaf')
The draws below stay inside these ranges and needn't reach their ends.
Inputs may be any that keep to these rules, and one draw needn't show every extreme that they name: Within each aligned block of 1024 tree positions, a permutation of that block's indices. `interactions`: entries of level l lie below 512/2^l and are equal over each aligned group of 2^l leaves; each names a node at level l that differs from the leaf's own ancestor (leaf // 2^l) by 2 or 3 in either direction. `coords`: the first coordinate of a point of leaf d lies in [d % 2, d % 2 + 1.5); the others in [0, 1).
All inputs are finite; a program needn't handle non-finite values.
Results may differ from the reference program's by a relative error of at most 0.00017.
Values sent between devices are 32-bit elements; how exact they have to be, the bound alone decides.
A program may use at most 64 MiB of HBM per device.

```python
import jax
import jax.numpy as jnp
from jax import lax

LEAF = 1024
RANK = 256
NCOL = 128
LEVELS = 3
SLOTS = 2
POINTS = 524288
TR_ROWS = 448
CP_ROWS = 960
N_LEAF = 512


def draw_coords(key, part):
    key = jax.random.fold_in(key, 5)
    first_key, second_key = jax.random.split(key)
    parity = (jnp.arange(POINTS) // LEAF % 2).astype(jnp.float32)
    along = parity + jax.random.uniform(first_key, (POINTS,), jnp.float32, 0.0, 1.5)
    across = jax.random.uniform(second_key, (2, POINTS), jnp.float32)
    return jnp.concatenate([along[None, :], across], axis=0)


def draw_permutation(key, part):
    key = jax.random.fold_in(key, 7)
    leaf_keys = jax.random.split(key, N_LEAF)
    shuffled = jax.vmap(lambda single: jax.random.permutation(single, LEAF))(leaf_keys)
    starts = (jnp.arange(N_LEAF, dtype=jnp.int32) * LEAF)[:, None]
    return (shuffled.astype(jnp.int32) + starts).reshape(POINTS)


def draw_interactions(key, part):
    key = jax.random.fold_in(key, 11)
    devices = jnp.arange(N_LEAF, dtype=jnp.int32)
    columns = []
    for tree_level in range(LEVELS + 1):
        level_key = jax.random.fold_in(key, tree_level)
        nodes = N_LEAF // 2 ** tree_level
        distance = jax.random.randint(level_key, (N_LEAF, SLOTS), 2, 4)
        signs = jax.random.randint(jax.random.fold_in(level_key, 1), (N_LEAF, SLOTS), 0, 2) * 2 - 1
        own_node = devices // 2 ** tree_level
        distance = distance[own_node]
        signs = signs[own_node]
        centre = own_node[:, None]
        to_last = centre == nodes - 3
        to_first = centre == 2
        signs = jnp.where(to_last, 1, jnp.where(to_first, -1, signs))
        distance = jnp.where(to_last | to_first, 2, distance)
        first = centre + signs * distance
        second = centre - signs * distance
        third = centre + signs * 2
        fourth = centre - signs * 2
        inside_first = (first >= 0) & (first < nodes)
        inside_second = (second >= 0) & (second < nodes)
        inside_third = (third >= 0) & (third < nodes)
        chosen = jnp.where(inside_first, first, jnp.where(inside_second, second, jnp.where(inside_third, third, fourth)))
        columns.append(chosen.astype(jnp.int32))
    return jnp.stack(columns, axis=1)


def levels(key, extent, pieces, least, high):
    factor_of, own = 1.0, jax.random.fold_in(key, 6)
    for axis_at, shards_of in pieces:
        heights = jnp.exp(jax.random.uniform(jax.random.fold_in(own, axis_at), (shards_of,), jnp.float32, least / len(pieces), high / len(pieces)))
        factor_of = factor_of * jnp.repeat(heights, extent[axis_at] // shards_of).reshape([-1 if axis == axis_at else 1 for axis in range(len(extent))])
    return factor_of


def bell_draw(key, dims, deviation, bound, cuts=(), held_as=jnp.bfloat16):
    values = deviation * jax.random.normal(key, dims, jnp.float32)
    if cuts:
        values = values * levels(key, dims, cuts, -0.22, 0.18)
    return jnp.clip(values, -bound, bound).astype(held_as)


def setup_inputs(seed: int = 0) -> dict:
    keys = jax.random.split(jax.random.key(seed), 8)
    values = bell_draw(keys[0], (POINTS, NCOL), 1.0, 6.0, ((0, 512),), jnp.float32)
    coords = draw_coords(jax.random.fold_in(keys[7], 71), 0)
    permutation = draw_permutation(jax.random.fold_in(keys[7], 71), 0)
    basis = bell_draw(keys[3], (POINTS, RANK), LEAF ** -0.5, 0.1875, ((0, 512),), jnp.float32)
    transfers = bell_draw(keys[4], (TR_ROWS * N_LEAF, RANK), RANK ** -0.5, 0.375, ((0, 512),), jnp.float32)
    couplings = bell_draw(keys[5], (CP_ROWS * N_LEAF, RANK), RANK ** -0.5, 0.375, ((0, 512),), jnp.float32)
    interactions = draw_interactions(jax.random.fold_in(keys[7], 71), 0)
    return dict(values=values, coords=coords, permutation=permutation, basis=basis, transfers=transfers, couplings=couplings, interactions=interactions)


def kernel_block(first_points, second_points):
    squared = (first_points[0][:, None] - second_points[0][None, :]) ** 2
    squared = squared + (first_points[1][:, None] - second_points[1][None, :]) ** 2
    squared = squared + (first_points[2][:, None] - second_points[2][None, :]) ** 2
    return jnp.exp(-8.0 * squared)


def reference(values, coords, permutation, basis, transfers, couplings, interactions):
    highest = lax.Precision.HIGHEST
    tree_values = values[permutation].reshape(N_LEAF, LEAF, NCOL)
    leaf_basis = basis.reshape(N_LEAF, LEAF, RANK)
    coeffs = [jnp.einsum("npr,npc->nrc", leaf_basis, tree_values, precision=highest)]
    blocks_tr = transfers.reshape(N_LEAF, TR_ROWS, RANK)
    blocks_cp = couplings.reshape(N_LEAF, CP_ROWS, RANK)

    def transfer_mats(tree_level):
        start = 0
        for lower in range(1, tree_level):
            start += RANK // 2 ** (lower - 1)
        count = RANK // 2 ** (tree_level - 1)
        return blocks_tr[:, start:start + count, :].reshape(N_LEAF // 2 ** (tree_level - 1), RANK, RANK)

    for tree_level in range(1, LEVELS + 1):
        mats = transfer_mats(tree_level)
        terms = jnp.einsum("krs,krc->ksc", mats, coeffs[-1], precision=highest)
        coeffs.append(terms.reshape(-1, 2, RANK, NCOL).sum(axis=1))

    local_parts = []
    start = 0
    for tree_level in range(LEVELS + 1):
        nodes = N_LEAF // 2 ** tree_level
        count = RANK // 2 ** tree_level
        total = jnp.zeros((nodes, RANK, NCOL), jnp.float32)
        for slot_index in range(SLOTS):
            mats = blocks_cp[:, start:start + count, :].reshape(nodes, RANK, RANK)
            start += count
            sources = interactions[::2 ** tree_level, tree_level, slot_index]
            picked = coeffs[tree_level][sources]
            total = total + jnp.einsum("nqr,nqc->nrc", mats, picked, precision=highest)
        local_parts.append(total * (2.0 ** (-tree_level / 2.0)))

    downward = local_parts[LEVELS]
    for tree_level in range(LEVELS, 0, -1):
        mats = transfer_mats(tree_level)
        parents = jnp.repeat(downward, 2, axis=0)
        downward = local_parts[tree_level - 1] + jnp.einsum("krs,ksc->krc", mats, parents, precision=highest)
    far_tree = jnp.einsum("npr,nrc->npc", leaf_basis, downward, precision=highest).reshape(POINTS, NCOL)
    far_field = jnp.zeros((POINTS, NCOL), jnp.float32).at[permutation].set(far_tree)

    leaf_points = coords.reshape(3, N_LEAF, LEAF)
    padded_points = jnp.concatenate([jnp.zeros((3, 1, LEAF), jnp.float32), leaf_points, jnp.zeros((3, 1, LEAF), jnp.float32)], axis=1)
    leaf_values = values.reshape(N_LEAF, LEAF, NCOL)
    padded_values = jnp.concatenate([jnp.zeros((1, LEAF, NCOL), jnp.float32), leaf_values, jnp.zeros((1, LEAF, NCOL), jnp.float32)], axis=0)

    def near_leaf(leaf_index):
        own_points = lax.dynamic_slice_in_dim(padded_points, leaf_index + 1, 1, axis=1)[:, 0, :]
        total = jnp.zeros((LEAF, NCOL), jnp.float32)
        for offset in (0, 1, 2):
            other_points = lax.dynamic_slice_in_dim(padded_points, leaf_index + offset, 1, axis=1)[:, 0, :]
            other_values = lax.dynamic_slice_in_dim(padded_values, leaf_index + offset, 1, axis=0)[0]
            total = total + jnp.dot(kernel_block(own_points, other_points), other_values, precision=highest)
        return total

    near_field = lax.map(near_leaf, jnp.arange(N_LEAF, dtype=jnp.int32)).reshape(POINTS, NCOL)
    return near_field + far_field
```

```python
import functools
import math

import jax
import jax.numpy as jnp
from jax import lax
from jax.experimental import pallas as pl
from jax.experimental.pallas import tpu as pltpu
from jax.sharding import PartitionSpec as P

LEAF = 1024
RANK = 256
NCOL = 128
N_LEAF = 512
ROWS = 256
MESH = pl.DeviceIdType.MESH
F32 = jnp.float32
BF16 = jnp.bfloat16
NT = (((1,), (1,)), ((), ()))
NN = (((1,), (0,)), ((), ()))
SCALE = math.sqrt(8.0 * math.log2(math.e))


def split(x):
    hi = x.astype(BF16)
    return hi, (x - hi.astype(F32)).astype(BF16)


def dot(a, b, dims=NN):
    return lax.dot_general(a, b, dims, preferred_element_type=F32)


def dot3(a, b, dims=NN):
    a_hi, a_lo = a
    b_hi, b_lo = b
    return dot(a_hi, b_hi, dims) + (dot(a_hi, b_lo, dims) + dot(a_lo, b_hi, dims))


def kernel(
    values, coords, perm, basis, transfers, couplings, inter, out,
    val, bas, e1, e2, e3, cpl, cs, pc, vst, nst, nv, nc, oh_b, bt_hi, bt_lo,
    c0, t1, t1r, c1, t2, t2r, t3, t3r, c2, c3, r0, r1, r2, r3,
    yh, yhr, h2, h2r, h3, h3r, f3, f1, y0,
    loc, snd, rcv,
):
    me = lax.axis_index("leaf")
    core = me % 2
    quarter = me % 4
    eighth = me % 8

    def at(offset):
        return (me + offset + N_LEAF) % N_LEAF

    p1 = me + 1 - 2 * core
    p2 = me + 2 - 4 * (me // 2 % 2)
    p4 = me + 4 - 8 * (me // 4 % 2)
    p6 = p2 + 4 - 8 * (me // 4 % 2)

    local = []

    def bring(src, dst):
        copy = pltpu.make_async_copy(src, dst, loc.at[len(local)])
        copy.start()
        local.append(copy)
        return copy

    e2_row = pl.multiple_of(core * 128, 128)
    e3_row = pl.multiple_of(quarter * 64, 64)
    get_basis = bring(basis, bas)
    get_values = bring(values, val)
    get_e1 = bring(transfers.at[pl.ds(0, 256)], e1)
    get_e2 = bring(transfers.at[pl.ds(256, 128)], e2.at[pl.ds(e2_row, 128)])
    get_e3 = bring(transfers.at[pl.ds(384, 64)], e3.at[pl.ds(e3_row, 64)])
    get_cpl = bring(couplings, cpl)

    barrier = pltpu.get_barrier_semaphore()
    greet = [at(o) for o in (1, -1, 2, -2, 4, -4, 8, -8, 24, -24)] + [p1, p2, p4, p6]
    for peer in greet:
        pl.semaphore_signal(barrier, inc=1, device_id=(peer,), device_id_type=MESH)

    cs[pl.ds(0, 3), :] = coords[...] * SCALE
    cs[pl.ds(3, 5), :] = jnp.zeros((5, LEAF), F32)
    pc[...] = cs[...].T

    pl.semaphore_wait(barrier, len(greet))

    used = []

    def send(src, dst, peer):
        index = len(used)
        copy = pltpu.make_async_remote_copy(
            src_ref=src, dst_ref=dst, send_sem=snd.at[index], recv_sem=rcv.at[index],
            device_id=(peer,), device_id_type=MESH,
        )
        copy.start()
        used.append(copy)
        return copy

    e3_own = e3.at[pl.ds(e3_row, 64)]
    e3_far = send(transfers.at[pl.ds(384, 64)], e3_own, p2)
    e3_near = send(transfers.at[pl.ds(384, 64)], e3_own, p1)
    e2_near = send(transfers.at[pl.ds(256, 128)], e2.at[pl.ds(e2_row, 128)], p1)
    n_up = send(values, nv.at[0], at(1))
    n_down = send(values, nv.at[1], at(-1))
    c_up = send(cs, nc.at[0], at(1))
    c_down = send(cs, nc.at[1], at(-1))

    get_basis.wait()
    b_hi, b_lo = split(bas[...])
    oh_b[:, :RANK] = b_hi
    oh_b[:, RANK:] = b_lo
    order = perm[...] % LEAF

    def place(i, carry):
        row = pl.multiple_of(i * ROWS, ROWS)
        point = lax.broadcasted_iota(jnp.int32, (ROWS, LEAF), 0) + row
        hot = jnp.where(point == order, 1.0, 0.0).astype(BF16)
        moved = dot(hot, oh_b[...])
        bt_hi[pl.ds(row, ROWS), :] = moved[:, :RANK].astype(BF16)
        bt_lo[pl.ds(row, ROWS), :] = moved[:, RANK:].astype(BF16)
        return carry

    lax.fori_loop(0, LEAF // ROWS, place, 0)
    get_values.wait()
    v_hi, v_lo = split(val[...])
    vst[:, :NCOL] = v_hi
    vst[:, NCOL:] = v_lo
    vt_hi, vt_lo = split(val[...].T)
    c0_t = dot3((vt_hi, vt_lo), (bt_hi[...], bt_lo[...]))
    c0[...] = c0_t
    s0_up = send(c0, r0.at[0], at(2))
    s0_down = send(c0, r0.at[2], at(-2))
    get_e1.wait()
    t1_t = dot3(split(c0_t), split(e1[...]))
    t1[...] = t1_t
    s1 = send(t1, t1r, p1)

    def near(block, points, scaled, first, count):
        def step(i, carry):
            row = pl.multiple_of(i * ROWS, ROWS)
            own = pc[pl.ds(row, ROWS), :]
            total = None
            for j in range(0, LEAF, 256):
                far = None
                for axis in range(3):
                    gap = own[:, axis:axis + 1] - points[axis:axis + 1, j:j + 256]
                    far = gap * gap if far is None else far + gap * gap
                k_hi, k_lo = split(jnp.exp2(-far))
                both = block[j:j + 256, :]
                term = dot(k_hi, both)
                part = term[:, :NCOL] + term[:, NCOL:] + dot(k_lo, both[:, :NCOL])
                total = part if total is None else total + part
            if scaled is None:
                out[pl.ds(row, ROWS), :] = total
            else:
                out[pl.ds(row, ROWS), :] += total * scaled
            return carry

        lax.fori_loop(first, first + count, step, 0)

    near(vst, cs, None, 0, 1)

    s1.wait_recv()
    c1_t = t1[...] + t1r[...]
    c1[...] = jnp.where(core == 0, c1_t[:, :128], c1_t[:, 128:])
    s2_up = send(c1, r1.at[0], at(4))
    s2_down = send(c1, r1.at[2], at(-4))
    get_e2.wait()
    e2_near.wait_recv()
    get_e3.wait()
    e3_far.wait_recv()
    other = pl.multiple_of((quarter + 2 - 4 * (quarter // 2)) * 64, 64)
    e3_relay = send(e3.at[pl.ds(other, 64)], e3.at[pl.ds(other, 64)], p1)
    t2_t = dot3(split(c1_t), split(e2[...]))
    t2[...] = t2_t.T
    u2 = send(t2.at[pl.ds(other, 64)], t2r, p2)
    e3_near.wait_recv()
    e3_relay.wait_recv()
    t3_t = dot3(split(t2_t), split(e3[...]))
    t3[...] = t3_t.T
    u3 = []
    for n, peer in enumerate((p2, p4, p6)):
        piece = pl.multiple_of(peer % 8 * 32, 32)
        u3.append(send(t3.at[pl.ds(piece, 32)], t3r.at[n], peer))

    near(vst, cs, None, 1, 1)

    for copy in u3:
        copy.wait_recv()
    c3[...] = (t3[pl.ds(pl.multiple_of(eighth * 32, 32), 32), :] + t3r[0]) + (t3r[1] + t3r[2])
    s4_up = send(c3, r3.at[1], at(24))
    s4_down = send(c3, r3.at[3], at(-24))
    u2.wait_recv()
    c2[...] = t2[pl.ds(pl.multiple_of(quarter * 64, 64), 64), :] + t2r[...]
    s3_up = send(c2, r2.at[0], at(8))
    s3_down = send(c2, r2.at[2], at(-8))

    near(vst, cs, None, 2, 2)

    s4_up.wait_recv()
    f4_down = send(r3.at[1], r3.at[0], at(-8))
    s4_down.wait_recv()
    f4_up = send(r3.at[3], r3.at[2], at(8))
    s3_up.wait_recv()
    f3_up = send(r2.at[0], r2.at[1], at(4))
    s3_down.wait_recv()
    f3_down = send(r2.at[2], r2.at[3], at(-4))
    s2_up.wait_recv()
    f2_up = send(r1.at[0], r1.at[1], at(2))
    s2_down.wait_recv()
    f2_down = send(r1.at[2], r1.at[3], at(-2))
    s0_up.wait_recv()
    f0_up = send(r0.at[0], r0.at[1], at(1))
    s0_down.wait_recv()
    f0_down = send(r0.at[2], r0.at[3], at(-1))

    n_up.wait_recv()
    c_up.wait_recv()
    w_hi, w_lo = split(nv[0])
    nst[0, :, :NCOL] = w_hi
    nst[0, :, NCOL:] = w_lo
    has_left = jnp.where(me > 0, 1.0, 0.0)
    has_right = jnp.where(me < N_LEAF - 1, 1.0, 0.0)
    near(nst.at[0], nc.at[0], has_left, 0, 4)

    def choose(buf, level, slot):
        delta = inter[slot, level] - me // 2 ** level
        return jnp.where(
            delta == -2, buf[0], jnp.where(delta == -3, buf[1], jnp.where(delta == 2, buf[2], buf[3]))
        )

    def halves(y, level):
        keep = pl.multiple_of(core * 64, 64)
        give = pl.multiple_of((1 - core) * 64, 64)
        yh[level - 1] = y
        return keep, send(yh.at[level - 1, pl.ds(give, 64)], yhr.at[level - 1], p1)

    get_cpl.wait()
    f4_down.wait_recv()
    f4_up.wait_recv()
    both3 = jnp.concatenate([choose(r3, 3, 0), choose(r3, 3, 1)], axis=0).T
    y3 = dot3(split(both3), split(cpl[pl.ds(896, 64), :])) * 2.0 ** -1.5
    keep, d3 = halves(y3, 3)
    f3_up.wait_recv()
    f3_down.wait_recv()
    both2 = jnp.concatenate([choose(r2, 2, 0), choose(r2, 2, 1)], axis=0).T
    y2 = dot3(split(both2), split(cpl[pl.ds(768, 128), :])) * 0.5
    keep, d2 = halves(y2, 2)

    d3.wait_recv()
    h3[...] = yh[2, pl.ds(keep, 64), :] + yhr[2]
    q3 = []
    for n, peer in enumerate((p2, p4, p6)):
        piece = pl.multiple_of(peer // 2 % 4 * 16, 16)
        q3.append(send(h3.at[pl.ds(piece, 16)], h3r.at[n], peer))
    d2.wait_recv()
    h2[...] = yh[1, pl.ds(keep, 64), :] + yhr[1]
    q2 = send(h2, h2r, p2)

    n_down.wait_recv()
    c_down.wait_recv()
    w_hi, w_lo = split(nv[1])
    nst[1, :, :NCOL] = w_hi
    nst[1, :, NCOL:] = w_lo
    near(nst.at[1], nc.at[1], has_right, 0, 2)

    for copy in q3:
        copy.wait_recv()
    mine = pl.multiple_of(me // 2 % 4 * 16, 16)
    f3[pl.ds(mine, 16), :] = (h3[pl.ds(mine, 16), :] + h3r[0]) + (h3r[1] + h3r[2])
    g3 = []
    for peer in (p2, p4, p6):
        g3.append(send(f3.at[pl.ds(mine, 16)], f3.at[pl.ds(mine, 16)], peer))

    f2_up.wait_recv()
    f2_down.wait_recv()
    both1 = jnp.concatenate([choose(r1, 1, 0), choose(r1, 1, 1)], axis=1)
    y1 = dot3(split(both1), split(cpl[pl.ds(512, 256), :])) * 2.0 ** -0.5
    keep, d1 = halves(y1, 1)
    f0_up.wait_recv()
    f0_down.wait_recv()
    both0 = jnp.concatenate([choose(r0, 0, 0), choose(r0, 0, 1)], axis=1)
    y0[...] = dot3(split(both0), split(cpl[pl.ds(0, 512), :]))

    near(nst.at[1], nc.at[1], has_right, 2, 2)

    q2.wait_recv()
    for copy in g3:
        copy.wait_recv()
    d1.wait_recv()
    f2_t = (h2[...] + h2r[...]) + dot3(split(f3[...]), split(e3[...]), NT)
    f1_half = (yh[0, pl.ds(keep, 64), :] + yhr[0]) + dot3(split(f2_t), split(e2[...]), NT)
    f1[pl.ds(keep, 64), :] = f1_half
    g1 = send(f1.at[pl.ds(keep, 64)], f1.at[pl.ds(keep, 64)], p1)
    g1.wait_recv()
    f0 = y0[...] + dot3(split(f1[...]), split(e1[...]), NT)
    f0_s = split(f0)

    def finish(i, carry):
        row = pl.multiple_of(i * ROWS, ROWS)
        rows = (bt_hi[pl.ds(row, ROWS), :], bt_lo[pl.ds(row, ROWS), :])
        out[pl.ds(row, ROWS), :] += dot3(rows, f0_s, NT)
        return carry

    lax.fori_loop(0, LEAF // ROWS, finish, 0)
    for copy in used:
        copy.wait_send()


def per_device(values, coords, permutation, basis, transfers, couplings, interactions):
    vmem = pl.BlockSpec(memory_space=pltpu.VMEM)
    smem = pl.BlockSpec(memory_space=pltpu.SMEM)
    hbm = pl.BlockSpec(memory_space=pl.ANY)

    def f32(*shape):
        return pltpu.VMEM(shape, F32)

    def b16(*shape):
        return pltpu.VMEM(shape, BF16)

    copies = 48
    return pl.pallas_call(
        kernel,
        out_shape=jax.ShapeDtypeStruct((LEAF, NCOL), F32),
        in_specs=[hbm, vmem, vmem, hbm, hbm, hbm, smem],
        out_specs=vmem,
        scratch_shapes=[
            f32(LEAF, NCOL), f32(LEAF, RANK), f32(256, 256), f32(256, 256), f32(256, 256),
            f32(960, 256), f32(8, LEAF), f32(LEAF, 8), b16(LEAF, 256), b16(2, LEAF, 256),
            f32(2, LEAF, NCOL), f32(2, 8, LEAF), b16(LEAF, 512), b16(LEAF, 256), b16(LEAF, 256),
            f32(128, 256), f32(128, 256), f32(128, 256), f32(128, 128),
            f32(256, 128), f32(64, 128), f32(256, 128), f32(3, 32, 128),
            f32(64, 128), f32(32, 128),
            f32(4, 128, 256), f32(4, 128, 128), f32(4, 64, 128), f32(4, 32, 128),
            f32(3, 128, 256), f32(3, 64, 256), f32(64, 256), f32(64, 256),
            f32(64, 256), f32(3, 16, 256), f32(64, 256), f32(128, 256), f32(128, 256),
            pltpu.SemaphoreType.DMA((6,)),
            pltpu.SemaphoreType.DMA((copies,)),
            pltpu.SemaphoreType.DMA((copies,)),
        ],
        compiler_params=pltpu.CompilerParams(
            collective_id=0, has_side_effects=True, vmem_limit_bytes=48 * 2 ** 20
        ),
        cost_estimate=pl.CostEstimate(
            flops=3 * 2 ** 30, bytes_accessed=4 * 2 ** 20, transcendentals=3 * 2 ** 20
        ),
    )(
        values, coords, permutation.reshape(1, LEAF), basis, transfers, couplings,
        interactions.transpose(0, 2, 1).reshape(2, 4),
    )


def solution(mesh):
    in_specs = (
        P("leaf", None),
        P(None, "leaf"),
        P("leaf"),
        P("leaf", None),
        P("leaf", None),
        P("leaf", None),
        P("leaf", None, None),
    )
    out_specs = P("leaf", None)
    return jax.shard_map(
        per_device, mesh=mesh, in_specs=in_specs, out_specs=out_specs, check_vma=False
    )
```

```python
import functools
import math

import jax
import jax.numpy as jnp
from jax import lax
from jax.experimental import pallas as pl
from jax.experimental.pallas import tpu as pltpu
from jax.sharding import PartitionSpec as P

LEAF = 1024
RANK = 256
NCOL = 128
N_LEAF = 512
ROWS = 256
MESH = pl.DeviceIdType.MESH
F32 = jnp.float32
BF16 = jnp.bfloat16
NT = (((1,), (1,)), ((), ()))
NN = (((1,), (0,)), ((), ()))
SCALE = math.sqrt(8.0 * math.log2(math.e))


def split(x):
    hi = x.astype(BF16)
    return hi, (x - hi.astype(F32)).astype(BF16)


def dot(a, b, dims=NN):
    return lax.dot_general(a, b, dims, preferred_element_type=F32)


def dot3(a, b, dims=NN):
    a_hi, a_lo = a
    b_hi, b_lo = b
    return dot(a_hi, b_hi, dims) + (dot(a_hi, b_lo, dims) + dot(a_lo, b_hi, dims))


def kernel(
    values, coords_in, perm_in, basis, transfers, couplings, inter, out,
    coords, perm,
    val, bas, e1, e2, e3, cp0, cw, cs, pc, vst, nst, nv, nc, oh_b, bt_hi, bt_lo,
    c0, t1, t1r, c1, t2, t2r, t3, t3r, c2, c3, r0, r1, r2, r3,
    h2, h2r, h3, h3r, f3, f1, y0, y1,
    loc, snd, rcv,
):
    me = lax.axis_index("leaf")
    core = me % 2
    quarter = me % 4
    pair = me // 2 % 2
    chip = me // 2 % 4

    def at(offset):
        return (me + offset + N_LEAF) % N_LEAF

    p1 = me + 1 - 2 * core
    p2 = me + 2 - 4 * (me // 2 % 2)
    p4 = me + 4 - 8 * (me // 4 % 2)
    p6 = p2 + 4 - 8 * (me // 4 % 2)
    p3 = p2 + 1 - 2 * core

    barrier = pltpu.get_barrier_semaphore()

    def inside(offset):
        return (me + offset >= 0) & (me + offset < N_LEAF)

    def greet(peer):
        pl.semaphore_signal(barrier, inc=1, device_id=(peer,), device_id_type=MESH)

    group = (p1, p2, p3, p4, p6)
    for peer in group:
        greet(peer)
    expected = len(group)
    for offset in (1, -1, 2, -2, 4, -4, 8, -8, 16, -16, 24, -24):
        pl.when(inside(offset))(functools.partial(greet, at(offset)))
        expected = expected + jnp.where(inside(offset), 1, 0)

    local = []

    def bring(src, dst):
        copy = pltpu.make_async_copy(src, dst, loc.at[len(local)])
        copy.start()
        local.append(copy)
        return copy

    e2_row = pl.multiple_of(core * 128, 128)
    e3_row = pl.multiple_of(quarter * 64, 64)
    get_coords = bring(coords_in, coords)
    get_perm = bring(perm_in, perm)
    get_basis = bring(basis, bas)
    get_values = bring(values, val)
    get_e1 = bring(transfers.at[pl.ds(0, 256)], e1)
    get_e2 = bring(transfers.at[pl.ds(256, 128)], e2.at[pl.ds(e2_row, 128)])
    get_e3 = bring(transfers.at[pl.ds(384, 64)], e3.at[pl.ds(e3_row, 64)])
    get_cp0 = bring(couplings.at[pl.ds(0, 512)], cp0)
    get_cw = bring(couplings.at[pl.ds(512, 448)], cw.at[core])

    get_coords.wait()
    cs[pl.ds(0, 3), :] = coords[...] * SCALE
    cs[pl.ds(3, 5), :] = jnp.zeros((5, LEAF), F32)
    pc[...] = cs[...].T

    get_basis.wait()
    b_hi, b_lo = split(bas[...])
    oh_b[:, :RANK] = b_hi
    oh_b[:, RANK:] = b_lo
    get_perm.wait()
    order = perm[...] % LEAF

    def place(i, carry):
        row = pl.multiple_of(i * ROWS, ROWS)
        point = lax.broadcasted_iota(jnp.int32, (ROWS, LEAF), 0) + row
        hot = jnp.where(point == order, 1.0, 0.0).astype(BF16)
        moved = dot(hot, oh_b[...])
        bt_hi[pl.ds(row, ROWS), :] = moved[:, :RANK].astype(BF16)
        bt_lo[pl.ds(row, ROWS), :] = moved[:, RANK:].astype(BF16)
        return carry

    lax.fori_loop(0, LEAF // ROWS, place, 0)
    get_values.wait()
    v_hi, v_lo = split(val[...])
    vst[:, :NCOL] = v_hi
    vst[:, NCOL:] = v_lo
    vt_hi, vt_lo = split(val[...].T)
    c0_t = dot3((vt_hi, vt_lo), (bt_hi[...], bt_lo[...]))
    c0[...] = c0_t
    get_e1.wait()
    t1_t = dot3(split(c0_t), split(e1[...]))
    t1[...] = t1_t
    get_e2.wait()
    get_e3.wait()
    get_cp0.wait()
    get_cw.wait()

    pl.semaphore_wait(barrier, expected)

    used = []

    class Sent:
        def __init__(self, copy, goes, comes):
            self.copy, self.goes, self.comes = copy, goes, comes

        def wait_recv(self):
            if self.comes is None:
                self.copy.wait_recv()
            else:
                pl.when(self.comes)(self.copy.wait_recv)

        def wait_send(self):
            if self.goes is None:
                self.copy.wait_send()
            else:
                pl.when(self.goes)(self.copy.wait_send)

    def send(src, dst, peer, goes=None, comes=None):
        index = len(used)
        copy = pltpu.make_async_remote_copy(
            src_ref=src, dst_ref=dst, send_sem=snd.at[index], recv_sem=rcv.at[index],
            device_id=(peer,), device_id_type=MESH,
        )
        if goes is None:
            copy.start()
        else:
            pl.when(goes)(copy.start)
        used.append(Sent(copy, goes, comes))
        return used[-1]

    def shift(src, dst, offset):
        return send(src, dst, at(offset), inside(offset), inside(-offset))

    def relay(src, dst, offset):
        return send(
            src, dst, at(offset), inside(-2 * offset) & inside(offset), inside(-3 * offset)
        )

    def share(piece):
        rows = pl.ds(piece * 256, 256)
        return (
            shift(values.at[rows], nv.at[0, rows], 1),
            shift(values.at[rows], nv.at[1, rows], -1),
        )

    def near(block, points, piece, fresh):
        j = piece * 256

        def step(i, carry):
            row = pl.multiple_of(i * ROWS, ROWS)
            own = pc[pl.ds(row, ROWS), :]
            far = None
            for axis in range(3):
                gap = own[:, axis:axis + 1] - points[axis:axis + 1, j:j + 256]
                far = gap * gap if far is None else far + gap * gap
            k_hi, k_lo = split(jnp.exp2(-far))
            both = block[j:j + 256, :]
            term = dot(k_hi, both)
            total = term[:, :NCOL] + term[:, NCOL:] + dot(k_lo, both[:, :NCOL])
            if fresh:
                out[pl.ds(row, ROWS), :] = total
            else:
                out[pl.ds(row, ROWS), :] += total
            return carry

        lax.fori_loop(0, LEAF // ROWS, step, 0)

    def near_side(side, sent, piece):
        def work():
            rows = pl.ds(piece * 256, 256)
            w_hi, w_lo = split(nv[side, rows, :])
            nst[side, rows, :NCOL] = w_hi
            nst[side, rows, NCOL:] = w_lo
            near(nst.at[side], nc.at[side], piece, False)

        sent[side].wait_recv()
        pl.when(inside(-1 if side == 0 else 1))(work)


    def choose(buf, level, slot):
        delta = inter[slot, level] - me // 2 ** level
        return jnp.where(
            delta == -2, buf[0], jnp.where(delta == -3, buf[1], jnp.where(delta == 2, buf[2], buf[3]))
        )

    def coupled(buf, level, first, count):
        both = jnp.concatenate([choose(buf, level, 0), choose(buf, level, 1)], axis=0).T
        rows = pl.ds(first, count)
        return (
            dot3(split(both[:64]), split(cw[0, rows, :]))
            + dot3(split(both[64:]), split(cw[1, rows, :]))
        ) * 2.0 ** (-level / 2.0)

    keep = pl.multiple_of(core * 64, 64)
    give = pl.multiple_of((1 - core) * 64, 64)
    e3_own = e3.at[pl.ds(e3_row, 64)]
    s1 = send(t1.at[pl.ds(give, 64)], t1r, p1)
    e2_near = send(transfers.at[pl.ds(256, 128)], e2.at[pl.ds(e2_row, 128)], p1)
    e3_far = send(transfers.at[pl.ds(384, 64)], e3_own, p2)
    e3_near = send(transfers.at[pl.ds(384, 64)], e3_own, p1)
    s0_up = shift(c0, r0.at[0], 2)
    s0_down = shift(c0, r0.at[2], -2)
    cw_near = send(couplings.at[pl.ds(512, 448)], cw.at[core], p1)
    c_up = shift(cs, nc.at[0], 1)
    c_down = shift(cs, nc.at[1], -1)
    near(vst, cs, 0, True)

    s1.wait_recv()
    c1_t = t1[pl.ds(keep, 64), :] + t1r[...]
    c1[...] = c1_t
    e2_near.wait_recv()
    t2_t = dot3(split(c1_t), split(e2[...]))
    t2_q = t2_t.T
    for b in range(2):
        t2[b] = jnp.concatenate([t2_q[b * 128:b * 128 + 64], t2_q[b * 128 + 64:b * 128 + 128]], axis=1)
    u2 = send(t2.at[1 - pair], t2r, p2)
    near(vst, cs, 1, False)
    e3_far.wait_recv()
    other = pl.multiple_of((quarter + 2 - 4 * (quarter // 2)) * 64, 64)
    e3_relay = send(e3.at[pl.ds(other, 64)], e3.at[pl.ds(other, 64)], p1)
    near(vst, cs, 2, False)
    e3_near.wait_recv()
    e3_relay.wait_recv()
    t3_t = dot3(split(t2_t), split(e3[...]))
    t3_q = t3_t.T
    for b in range(4):
        t3[b] = jnp.concatenate([t3_q[b * 64:b * 64 + 32], t3_q[b * 64 + 32:b * 64 + 64]], axis=1)
    u3 = []
    for n, peer in enumerate((p2, p4, p6)):
        u3.append(send(t3.at[peer // 2 % 4], t3r.at[n], peer))

    s2_up = shift(c1, r1.at[0], 4)
    s2_down = shift(c1, r1.at[2], -4)
    near(vst, cs, 3, False)
    s0_up.wait_recv()
    f0_up = relay(r0.at[0], r0.at[1], 1)
    s0_down.wait_recv()
    f0_down = relay(r0.at[2], r0.at[3], -1)
    u2.wait_recv()
    c2[...] = t2[pair] + t2r[...]
    for copy in u3:
        copy.wait_recv()
    c3[...] = (t3[chip] + t3r[0]) + (t3r[1] + t3r[2])
    s4 = [
        shift(c3, r3.at[0], 16), shift(c3, r3.at[2], -16),
        shift(c3, r3.at[1], 24), shift(c3, r3.at[3], -24),
    ]

    s3_up = shift(c2, r2.at[0], 8)
    s3_down = shift(c2, r2.at[2], -8)
    v0 = share(0)
    s2_up.wait_recv()
    f2_up = relay(r1.at[0], r1.at[1], 2)
    s2_down.wait_recv()
    f2_down = relay(r1.at[2], r1.at[3], -2)
    f0_up.wait_recv()
    f0_down.wait_recv()
    both0 = jnp.concatenate([choose(r0, 0, 0), choose(r0, 0, 1)], axis=1)
    y0[...] = dot3(split(both0), split(cp0[...]))

    s3_up.wait_recv()
    f3_up = relay(r2.at[0], r2.at[1], 4)
    s3_down.wait_recv()
    f3_down = relay(r2.at[2], r2.at[3], -4)
    c_up.wait_recv()
    c_down.wait_recv()
    cw_near.wait_recv()
    near_side(0, v0, 0)
    for copy in s4:
        copy.wait_recv()
    h3[...] = coupled(r3, 3, 384, 64)
    q3 = []
    for n, peer in enumerate((p2, p4, p6)):
        piece = pl.multiple_of(peer // 2 % 4 * 16, 16)
        q3.append(send(h3.at[pl.ds(piece, 16)], h3r.at[n], peer))

    v1 = share(1)
    v2 = share(2)
    near_side(1, v0, 0)
    f3_up.wait_recv()
    f3_down.wait_recv()
    h2[...] = coupled(r2, 2, 256, 128)
    q2 = send(h2, h2r, p2)
    f2_up.wait_recv()
    f2_down.wait_recv()
    both1 = jnp.concatenate([choose(r1, 1, 0), choose(r1, 1, 1)], axis=1)
    rows1 = jnp.concatenate(
        [cw[0, pl.ds(0, 128), :], cw[1, pl.ds(0, 128), :], cw[0, pl.ds(128, 128), :], cw[1, pl.ds(128, 128), :]],
        axis=0,
    )
    y1[...] = dot3(split(both1), split(rows1)) * 2.0 ** -0.5
    for copy in q3:
        copy.wait_recv()
    mine = pl.multiple_of(chip * 16, 16)
    f3[pl.ds(mine, 16), :] = (h3[pl.ds(mine, 16), :] + h3r[0]) + (h3r[1] + h3r[2])
    g3 = []
    for peer in (p2, p4, p6):
        g3.append(send(f3.at[pl.ds(mine, 16)], f3.at[pl.ds(mine, 16)], peer))

    v3 = share(3)
    near_side(0, v1, 1)
    near_side(1, v1, 1)
    near_side(0, v2, 2)
    near_side(1, v2, 2)
    q2.wait_recv()
    for copy in g3:
        copy.wait_recv()
    f2_t = (h2[...] + h2r[...]) + dot3(split(f3[...]), split(e3[...]), NT)
    f1_half = y1[...] + dot3(split(f2_t), split(e2[...]), NT)
    f1[pl.ds(keep, 64), :] = f1_half
    g1 = send(f1.at[pl.ds(keep, 64)], f1.at[pl.ds(keep, 64)], p1)
    near_side(0, v3, 3)
    near_side(1, v3, 3)
    g1.wait_recv()
    f0 = y0[...] + dot3(split(f1[...]), split(e1[...]), NT)
    f0_s = split(f0)

    def finish(i, carry):
        row = pl.multiple_of(i * ROWS, ROWS)
        rows = (bt_hi[pl.ds(row, ROWS), :], bt_lo[pl.ds(row, ROWS), :])
        out[pl.ds(row, ROWS), :] += dot3(rows, f0_s, NT)
        return carry

    lax.fori_loop(0, LEAF // ROWS, finish, 0)
    for copy in used:
        copy.wait_send()


def per_device(values, coords, permutation, basis, transfers, couplings, interactions):
    vmem = pl.BlockSpec(memory_space=pltpu.VMEM)
    smem = pl.BlockSpec(memory_space=pltpu.SMEM)
    hbm = pl.BlockSpec(memory_space=pltpu.HBM)

    def f32(*shape):
        return pltpu.VMEM(shape, F32)

    def b16(*shape):
        return pltpu.VMEM(shape, BF16)

    copies = 64
    return pl.pallas_call(
        kernel,
        out_shape=jax.ShapeDtypeStruct((LEAF, NCOL), F32),
        in_specs=[hbm, hbm, hbm, hbm, hbm, hbm, smem],
        out_specs=vmem,
        scratch_shapes=[
            f32(3, LEAF), pltpu.VMEM((1, LEAF), jnp.int32),
            f32(LEAF, NCOL), f32(LEAF, RANK), f32(256, 256), f32(256, 256), f32(256, 256),
            f32(512, 256), f32(2, 448, 256), f32(8, LEAF), f32(LEAF, 8), b16(LEAF, 256), b16(2, LEAF, 256),
            f32(2, LEAF, NCOL), f32(2, 8, LEAF), b16(LEAF, 512), b16(LEAF, 256), b16(LEAF, 256),
            f32(128, 256), f32(128, 256), f32(64, 256), f32(64, 256),
            f32(2, 64, 128), f32(64, 128), f32(4, 32, 128), f32(3, 32, 128),
            f32(64, 128), f32(32, 128),
            f32(4, 128, 256), f32(4, 64, 256), f32(4, 64, 128), f32(4, 32, 128),
            f32(64, 256), f32(64, 256), f32(64, 256), f32(3, 16, 256), f32(64, 256),
            f32(128, 256), f32(128, 256), f32(64, 256),
            pltpu.SemaphoreType.DMA((9,)),
            pltpu.SemaphoreType.DMA((copies,)),
            pltpu.SemaphoreType.DMA((copies,)),
        ],
        compiler_params=pltpu.CompilerParams(
            collective_id=0, has_side_effects=True, vmem_limit_bytes=63 * 2 ** 20
        ),
        cost_estimate=pl.CostEstimate(
            flops=3 * 2 ** 30, bytes_accessed=4 * 2 ** 20, transcendentals=3 * 2 ** 20
        ),
    )(
        values, coords, permutation.reshape(1, LEAF), basis, transfers, couplings,
        interactions.transpose(0, 2, 1).reshape(2, 4),
    )


def solution(mesh):
    in_specs = (
        P("leaf", None),
        P(None, "leaf"),
        P("leaf"),
        P("leaf", None),
        P("leaf", None),
        P("leaf", None),
        P("leaf", None, None),
    )
    out_specs = P("leaf", None)
    return jax.shard_map(
        per_device, mesh=mesh, in_specs=in_specs, out_specs=out_specs, check_vma=False
    )
```

```python
import functools
import math

import jax
import jax.numpy as jnp
from jax import lax
from jax.experimental import pallas as pl
from jax.experimental.pallas import tpu as pltpu
from jax.sharding import PartitionSpec as P

LEAF = 1024
RANK = 256
NCOL = 128
N_LEAF = 512
ROWS = 256
MESH = pl.DeviceIdType.MESH
F32 = jnp.float32
BF16 = jnp.bfloat16
NT = (((1,), (1,)), ((), ()))
NN = (((1,), (0,)), ((), ()))
SCALE = math.sqrt(8.0 * math.log2(math.e))


def split(x):
    hi = x.astype(BF16)
    return hi, (x - hi.astype(F32)).astype(BF16)


def dot(a, b, dims=NN):
    return lax.dot_general(a, b, dims, preferred_element_type=F32)


def dot3(a, b, dims=NN):
    a_hi, a_lo = a
    b_hi, b_lo = b
    return dot(a_hi, b_hi, dims) + (dot(a_hi, b_lo, dims) + dot(a_lo, b_hi, dims))


def kernel(
    values, coords_in, perm_in, basis, transfers, couplings, inter, out,
    coords, perm,
    val, bas, e1, e2, e3, cp0, cw, cs, pc, pb, vst, nst, nv, nc, oh_b, bt_hi, bt_lo,
    c0, t1, t1r, c1, t2, t2r, t3, t3r, c2, c3, r0, r1, r2, r3,
    h2, h2r, h3, h3r, f3, f1, y0, y1,
    loc, snd, rcv,
):
    me = lax.axis_index("leaf")
    core = me % 2
    quarter = me % 4
    pair = me // 2 % 2
    chip = me // 2 % 4

    def at(offset):
        return (me + offset + N_LEAF) % N_LEAF

    p1 = me + 1 - 2 * core
    p2 = me + 2 - 4 * (me // 2 % 2)
    p4 = me + 4 - 8 * (me // 4 % 2)
    p6 = p2 + 4 - 8 * (me // 4 % 2)
    p3 = p2 + 1 - 2 * core

    barrier = pltpu.get_barrier_semaphore()

    def inside(offset):
        return (me + offset >= 0) & (me + offset < N_LEAF)

    def greet(peer):
        pl.semaphore_signal(barrier, inc=1, device_id=(peer,), device_id_type=MESH)

    group = (p1, p2, p3, p4, p6)
    for peer in group:
        greet(peer)
    expected = len(group)
    for offset in (1, -1, 2, -2, 4, -4, 8, -8, 16, -16, 24, -24):
        pl.when(inside(offset))(functools.partial(greet, at(offset)))
        expected = expected + jnp.where(inside(offset), 1, 0)

    local = []

    def bring(src, dst):
        copy = pltpu.make_async_copy(src, dst, loc.at[len(local)])
        copy.start()
        local.append(copy)
        return copy

    e2_row = pl.multiple_of(core * 128, 128)
    e3_row = pl.multiple_of(quarter * 64, 64)
    get_coords = bring(coords_in, coords)
    get_perm = bring(perm_in, perm)
    get_basis = bring(basis, bas)
    get_values = bring(values, val)
    get_e1 = bring(transfers.at[pl.ds(0, 256)], e1)
    get_e2 = bring(transfers.at[pl.ds(256, 128)], e2.at[pl.ds(e2_row, 128)])
    get_e3 = bring(transfers.at[pl.ds(384, 64)], e3.at[pl.ds(e3_row, 64)])
    get_cp0 = bring(couplings.at[pl.ds(0, 512)], cp0)
    get_cw = bring(couplings.at[pl.ds(512, 448)], cw.at[core])

    get_coords.wait()
    cs[pl.ds(0, 3), :] = coords[...] * SCALE
    cs[pl.ds(3, 5), :] = jnp.zeros((5, LEAF), F32)
    pc[...] = cs[...].T

    get_basis.wait()
    b_hi, b_lo = split(bas[...])
    oh_b[:, :RANK] = b_hi
    oh_b[:, RANK:] = b_lo
    get_perm.wait()
    order = perm[...] % LEAF

    def place(i, carry):
        row = pl.multiple_of(i * ROWS, ROWS)
        point = lax.broadcasted_iota(jnp.int32, (ROWS, LEAF), 0) + row
        hot = jnp.where(point == order, 1.0, 0.0).astype(BF16)
        moved = dot(hot, oh_b[...])
        bt_hi[pl.ds(row, ROWS), :] = moved[:, :RANK].astype(BF16)
        bt_lo[pl.ds(row, ROWS), :] = moved[:, RANK:].astype(BF16)
        return carry

    lax.fori_loop(0, LEAF // ROWS, place, 0)
    pl.semaphore_wait(barrier, expected)

    used = []

    class Sent:
        def __init__(self, copy, goes, comes):
            self.copy, self.goes, self.comes = copy, goes, comes

        def wait_recv(self):
            if self.comes is None:
                self.copy.wait_recv()
            else:
                pl.when(self.comes)(self.copy.wait_recv)

        def wait_send(self):
            if self.goes is None:
                self.copy.wait_send()
            else:
                pl.when(self.goes)(self.copy.wait_send)

    def send(src, dst, peer, goes=None, comes=None):
        index = len(used)
        copy = pltpu.make_async_remote_copy(
            src_ref=src, dst_ref=dst, send_sem=snd.at[index], recv_sem=rcv.at[index],
            device_id=(peer,), device_id_type=MESH,
        )
        if goes is None:
            copy.start()
        else:
            pl.when(goes)(copy.start)
        used.append(Sent(copy, goes, comes))
        return used[-1]

    def shift(src, dst, offset):
        return send(src, dst, at(offset), inside(offset), inside(-offset))

    def relay(src, dst, offset):
        return send(
            src, dst, at(offset), inside(-2 * offset) & inside(offset), inside(-3 * offset)
        )

    def share(piece):
        rows = pl.ds(piece * 256, 256)
        return (
            shift(values.at[rows], nv.at[0, rows], 1),
            shift(values.at[rows], nv.at[1, rows], -1),
        )

    def near(block, points, piece, fresh):
        j = piece * 256

        def step(i, carry):
            row = pl.multiple_of(i * ROWS, ROWS)
            far = None
            for axis in range(3):
                own = pb[axis, pl.ds(row, ROWS), :]
                gap = jnp.concatenate([own, own], axis=1) - points[axis:axis + 1, j:j + 256]
                far = gap * gap if far is None else far + gap * gap
            k_hi, k_lo = split(jnp.exp2(-far))
            both = block[j:j + 256, :]
            term = dot(k_hi, both)
            total = term[:, :NCOL] + term[:, NCOL:] + dot(k_lo, both[:, :NCOL])
            if fresh:
                out[pl.ds(row, ROWS), :] = total
            else:
                out[pl.ds(row, ROWS), :] += total
            return carry

        lax.fori_loop(0, LEAF // ROWS, step, 0)

    def near_side(side, sent, piece):
        def work():
            rows = pl.ds(piece * 256, 256)
            w_hi, w_lo = split(nv[side, rows, :])
            nst[side, rows, :NCOL] = w_hi
            nst[side, rows, NCOL:] = w_lo
            near(nst.at[side], nc.at[side], piece, False)

        sent[side].wait_recv()
        pl.when(inside(-1 if side == 0 else 1))(work)


    def choose(buf, level, slot):
        delta = inter[slot, level] - me // 2 ** level
        return jnp.where(
            delta == -2, buf[0], jnp.where(delta == -3, buf[1], jnp.where(delta == 2, buf[2], buf[3]))
        )

    def coupled(buf, level, first, count):
        both = jnp.concatenate([choose(buf, level, 0), choose(buf, level, 1)], axis=0).T
        rows = pl.ds(first, count)
        return (
            dot3(split(both[:64]), split(cw[0, rows, :]))
            + dot3(split(both[64:]), split(cw[1, rows, :]))
        ) * 2.0 ** (-level / 2.0)

    keep = pl.multiple_of(core * 64, 64)
    give = pl.multiple_of((1 - core) * 64, 64)
    e3_own = e3.at[pl.ds(e3_row, 64)]
    e3_far = send(transfers.at[pl.ds(384, 64)], e3_own, p2)
    e3_near = send(transfers.at[pl.ds(384, 64)], e3_own, p1)
    e2_near = send(transfers.at[pl.ds(256, 128)], e2.at[pl.ds(e2_row, 128)], p1)
    c_up = shift(cs, nc.at[0], 1)
    c_down = shift(cs, nc.at[1], -1)
    v0 = share(0)

    get_values.wait()
    v_hi, v_lo = split(val[...])
    vst[:, :NCOL] = v_hi
    vst[:, NCOL:] = v_lo
    vt_hi, vt_lo = split(val[...].T)
    c0_t = dot3((vt_hi, vt_lo), (bt_hi[...], bt_lo[...]))
    c0[...] = c0_t
    get_e1.wait()
    t1_t = dot3(split(c0_t), split(e1[...]))
    t1[...] = t1_t
    get_e2.wait()
    get_e3.wait()

    s1 = send(t1.at[pl.ds(give, 64)], t1r, p1)
    s0_up = shift(c0, r0.at[0], 2)
    s0_down = shift(c0, r0.at[2], -2)
    cw_near = send(couplings.at[pl.ds(512, 448)], cw.at[core], p1)
    for axis in range(3):
        pb[axis] = jnp.broadcast_to(pc[:, axis:axis + 1], (LEAF, NCOL))
    near(vst, cs, 0, True)

    s1.wait_recv()
    c1_t = t1[pl.ds(keep, 64), :] + t1r[...]
    c1[...] = c1_t
    e2_near.wait_recv()
    t2_t = dot3(split(c1_t), split(e2[...]))
    t2_q = t2_t.T
    for b in range(2):
        t2[b] = jnp.concatenate([t2_q[b * 128:b * 128 + 64], t2_q[b * 128 + 64:b * 128 + 128]], axis=1)
    u2 = send(t2.at[1 - pair], t2r, p2)
    near(vst, cs, 1, False)
    e3_far.wait_recv()
    other = pl.multiple_of((quarter + 2 - 4 * (quarter // 2)) * 64, 64)
    e3_relay = send(e3.at[pl.ds(other, 64)], e3.at[pl.ds(other, 64)], p1)
    near(vst, cs, 2, False)
    e3_near.wait_recv()
    e3_relay.wait_recv()
    t3_t = dot3(split(t2_t), split(e3[...]))
    t3_q = t3_t.T
    for b in range(4):
        t3[b] = jnp.concatenate([t3_q[b * 64:b * 64 + 32], t3_q[b * 64 + 32:b * 64 + 64]], axis=1)
    u3 = []
    for n, peer in enumerate((p2, p4, p6)):
        u3.append(send(t3.at[peer // 2 % 4], t3r.at[n], peer))

    s2_up = shift(c1, r1.at[0], 4)
    s2_down = shift(c1, r1.at[2], -4)
    near(vst, cs, 3, False)
    s0_up.wait_recv()
    f0_up = relay(r0.at[0], r0.at[1], 1)
    s0_down.wait_recv()
    f0_down = relay(r0.at[2], r0.at[3], -1)
    u2.wait_recv()
    c2[...] = t2[pair] + t2r[...]
    for copy in u3:
        copy.wait_recv()
    c3[...] = (t3[chip] + t3r[0]) + (t3r[1] + t3r[2])
    s4 = [
        shift(c3, r3.at[0], 16), shift(c3, r3.at[2], -16),
        shift(c3, r3.at[1], 24), shift(c3, r3.at[3], -24),
    ]

    s3_up = shift(c2, r2.at[0], 8)
    s3_down = shift(c2, r2.at[2], -8)
    c_up.wait_recv()
    c_down.wait_recv()
    get_cw.wait()
    cw_near.wait_recv()
    near_side(0, v0, 0)
    near_side(1, v0, 0)
    s2_up.wait_recv()
    f2_up = relay(r1.at[0], r1.at[1], 2)
    s2_down.wait_recv()
    f2_down = relay(r1.at[2], r1.at[3], -2)
    f0_up.wait_recv()
    f0_down.wait_recv()
    both0 = jnp.concatenate([choose(r0, 0, 0), choose(r0, 0, 1)], axis=1)
    get_cp0.wait()
    y0[...] = dot3(split(both0), split(cp0[...]))

    v1 = share(1)
    s3_up.wait_recv()
    f3_up = relay(r2.at[0], r2.at[1], 4)
    s3_down.wait_recv()
    f3_down = relay(r2.at[2], r2.at[3], -4)
    for copy in s4:
        copy.wait_recv()
    h3[...] = coupled(r3, 3, 384, 64)
    q3 = []
    for n, peer in enumerate((p2, p4, p6)):
        piece = pl.multiple_of(peer // 2 % 4 * 16, 16)
        q3.append(send(h3.at[pl.ds(piece, 16)], h3r.at[n], peer))

    v2 = share(2)
    near_side(0, v1, 1)
    f3_up.wait_recv()
    f3_down.wait_recv()
    h2[...] = coupled(r2, 2, 256, 128)
    q2 = send(h2, h2r, p2)
    f2_up.wait_recv()
    f2_down.wait_recv()
    both1 = jnp.concatenate([choose(r1, 1, 0), choose(r1, 1, 1)], axis=1)
    rows1 = jnp.concatenate(
        [cw[0, pl.ds(0, 128), :], cw[1, pl.ds(0, 128), :], cw[0, pl.ds(128, 128), :], cw[1, pl.ds(128, 128), :]],
        axis=0,
    )
    y1[...] = dot3(split(both1), split(rows1)) * 2.0 ** -0.5
    for copy in q3:
        copy.wait_recv()
    mine = pl.multiple_of(chip * 16, 16)
    f3[pl.ds(mine, 16), :] = (h3[pl.ds(mine, 16), :] + h3r[0]) + (h3r[1] + h3r[2])
    g3 = []
    for peer in (p2, p4, p6):
        g3.append(send(f3.at[pl.ds(mine, 16)], f3.at[pl.ds(mine, 16)], peer))

    v3 = share(3)
    near_side(1, v1, 1)
    near_side(0, v2, 2)
    near_side(1, v2, 2)
    q2.wait_recv()
    for copy in g3:
        copy.wait_recv()
    f2_t = (h2[...] + h2r[...]) + dot3(split(f3[...]), split(e3[...]), NT)
    f1_half = y1[...] + dot3(split(f2_t), split(e2[...]), NT)
    f1[pl.ds(keep, 64), :] = f1_half
    g1 = send(f1.at[pl.ds(keep, 64)], f1.at[pl.ds(keep, 64)], p1)
    near_side(0, v3, 3)
    near_side(1, v3, 3)
    g1.wait_recv()
    f0 = y0[...] + dot3(split(f1[...]), split(e1[...]), NT)
    f0_hi, f0_lo = split(f0.T)
    f0_both = jnp.concatenate([f0_hi, f0_lo], axis=1)

    def finish(i, carry):
        row = pl.multiple_of(i * ROWS, ROWS)
        first = dot(bt_hi[pl.ds(row, ROWS), :], f0_both)
        second = dot(bt_lo[pl.ds(row, ROWS), :], f0_hi)
        out[pl.ds(row, ROWS), :] += first[:, :NCOL] + (first[:, NCOL:] + second)
        return carry

    lax.fori_loop(0, LEAF // ROWS, finish, 0)
    for copy in used:
        copy.wait_send()


def per_device(values, coords, permutation, basis, transfers, couplings, interactions):
    vmem = pl.BlockSpec(memory_space=pltpu.VMEM)
    smem = pl.BlockSpec(memory_space=pltpu.SMEM)
    hbm = pl.BlockSpec(memory_space=pltpu.HBM)

    def f32(*shape):
        return pltpu.VMEM(shape, F32)

    def b16(*shape):
        return pltpu.VMEM(shape, BF16)

    copies = 64
    return pl.pallas_call(
        kernel,
        out_shape=jax.ShapeDtypeStruct((LEAF, NCOL), F32),
        in_specs=[hbm, hbm, hbm, hbm, hbm, hbm, smem],
        out_specs=vmem,
        scratch_shapes=[
            f32(3, LEAF), pltpu.VMEM((1, LEAF), jnp.int32),
            f32(LEAF, NCOL), f32(LEAF, RANK), f32(256, 256), f32(256, 256), f32(256, 256),
            f32(512, 256), f32(2, 448, 256), f32(8, LEAF), f32(LEAF, 8), f32(3, LEAF, NCOL), b16(LEAF, 256), b16(2, LEAF, 256),
            f32(2, LEAF, NCOL), f32(2, 8, LEAF), b16(LEAF, 512), b16(LEAF, 256), b16(LEAF, 256),
            f32(128, 256), f32(128, 256), f32(64, 256), f32(64, 256),
            f32(2, 64, 128), f32(64, 128), f32(4, 32, 128), f32(3, 32, 128),
            f32(64, 128), f32(32, 128),
            f32(4, 128, 256), f32(4, 64, 256), f32(4, 64, 128), f32(4, 32, 128),
            f32(64, 256), f32(64, 256), f32(64, 256), f32(3, 16, 256), f32(64, 256),
            f32(128, 256), f32(128, 256), f32(64, 256),
            pltpu.SemaphoreType.DMA((9,)),
            pltpu.SemaphoreType.DMA((copies,)),
            pltpu.SemaphoreType.DMA((copies,)),
        ],
        compiler_params=pltpu.CompilerParams(
            collective_id=0, has_side_effects=True, vmem_limit_bytes=63 * 2 ** 20
        ),
        cost_estimate=pl.CostEstimate(
            flops=3 * 2 ** 30, bytes_accessed=4 * 2 ** 20, transcendentals=3 * 2 ** 20
        ),
    )(
        values, coords, permutation.reshape(1, LEAF), basis, transfers, couplings,
        interactions.transpose(0, 2, 1).reshape(2, 4),
    )


def solution(mesh):
    in_specs = (
        P("leaf", None),
        P(None, "leaf"),
        P("leaf"),
        P("leaf", None),
        P("leaf", None),
        P("leaf", None),
        P("leaf", None, None),
    )
    out_specs = P("leaf", None)
    return jax.shard_map(
        per_device, mesh=mesh, in_specs=in_specs, out_specs=out_specs, check_vma=False
    )
```

```python
import functools
import math

import jax
import jax.numpy as jnp
from jax import lax
from jax.experimental import pallas as pl
from jax.experimental.pallas import tpu as pltpu
from jax.sharding import PartitionSpec as P

LEAF = 1024
RANK = 256
NCOL = 128
N_LEAF = 512
ROWS = 256
MESH = pl.DeviceIdType.MESH
F32 = jnp.float32
BF16 = jnp.bfloat16
NT = (((1,), (1,)), ((), ()))
NN = (((1,), (0,)), ((), ()))
SCALE = math.sqrt(8.0 * math.log2(math.e))


def split(x):
    hi = x.astype(BF16)
    return hi, (x - hi.astype(F32)).astype(BF16)


def dot(a, b, dims=NN):
    return lax.dot_general(a, b, dims, preferred_element_type=F32)


def dot3(a, b, dims=NN):
    a_hi, a_lo = a
    b_hi, b_lo = b
    return dot(a_hi, b_hi, dims) + (dot(a_hi, b_lo, dims) + dot(a_lo, b_hi, dims))


def kernel(
    values, coords_in, perm_in, basis, transfers, couplings, inter, out,
    coords, perm,
    val, bas, e1, e2, e3, cp0, cw, cs, pc, pb, vst, nst, nv, nc, oh_b, bt_hi, bt_lo,
    c0, t1, t1r, c1, t2, t2r, t3, t3r, c2, c3, r0, r1, r2, r3,
    h2, h2r, h3, h3r, f3, f1, y0, y1, et,
    loc, snd, rcv,
):
    me = lax.axis_index("leaf")
    core = me % 2
    quarter = me % 4
    pair = me // 2 % 2
    chip = me // 2 % 4

    def at(offset):
        return (me + offset + N_LEAF) % N_LEAF

    p1 = me + 1 - 2 * core
    p2 = me + 2 - 4 * (me // 2 % 2)
    p4 = me + 4 - 8 * (me // 4 % 2)
    p6 = p2 + 4 - 8 * (me // 4 % 2)
    p3 = p2 + 1 - 2 * core

    barrier = pltpu.get_barrier_semaphore()

    def inside(offset):
        return (me + offset >= 0) & (me + offset < N_LEAF)

    def greet(peer):
        pl.semaphore_signal(barrier, inc=1, device_id=(peer,), device_id_type=MESH)

    group = (p1, p2, p3, p4, p6)
    for peer in group:
        greet(peer)
    expected = len(group)
    for offset in (1, -1, 2, -2, 4, -4, 8, -8, 16, -16, 24, -24):
        pl.when(inside(offset))(functools.partial(greet, at(offset)))
        expected = expected + jnp.where(inside(offset), 1, 0)

    local = []

    def bring(src, dst):
        copy = pltpu.make_async_copy(src, dst, loc.at[len(local)])
        copy.start()
        local.append(copy)
        return copy

    e2_row = pl.multiple_of(core * 128, 128)
    e3_row = pl.multiple_of(quarter * 64, 64)
    get_coords = bring(coords_in, coords)
    get_perm = bring(perm_in, perm)
    get_basis = bring(basis, bas)
    get_values = bring(values, val)
    get_e1 = bring(transfers.at[pl.ds(0, 256)], e1)
    get_e2 = bring(transfers.at[pl.ds(256, 128)], e2.at[pl.ds(e2_row, 128)])
    get_e3 = bring(transfers.at[pl.ds(384, 64)], e3.at[pl.ds(e3_row, 64)])
    get_cp0 = bring(couplings.at[pl.ds(0, 512)], cp0)
    get_cw = bring(couplings.at[pl.ds(512, 448)], cw.at[core])

    get_coords.wait()
    cs[pl.ds(0, 3), :] = coords[...] * SCALE
    cs[pl.ds(3, 5), :] = jnp.zeros((5, LEAF), F32)
    pc[...] = cs[...].T

    get_basis.wait()
    b_hi, b_lo = split(bas[...])
    oh_b[:, :RANK] = b_hi
    oh_b[:, RANK:] = b_lo
    get_perm.wait()
    order = perm[...] % LEAF

    def place(i, carry):
        row = pl.multiple_of(i * ROWS, ROWS)
        point = lax.broadcasted_iota(jnp.int32, (ROWS, LEAF), 0) + row
        hot = jnp.where(point == order, 1.0, 0.0).astype(BF16)
        moved = dot(hot, oh_b[...])
        bt_hi[pl.ds(row, ROWS), :] = moved[:, :RANK].astype(BF16)
        bt_lo[pl.ds(row, ROWS), :] = moved[:, RANK:].astype(BF16)
        return carry

    lax.fori_loop(0, LEAF // ROWS, place, 0)
    pl.semaphore_wait(barrier, expected)

    used = []

    class Sent:
        def __init__(self, copy, goes, comes):
            self.copy, self.goes, self.comes = copy, goes, comes

        def wait_recv(self):
            if self.comes is None:
                self.copy.wait_recv()
            else:
                pl.when(self.comes)(self.copy.wait_recv)

        def wait_send(self):
            if self.goes is None:
                self.copy.wait_send()
            else:
                pl.when(self.goes)(self.copy.wait_send)

    def send(src, dst, peer, goes=None, comes=None):
        index = len(used)
        copy = pltpu.make_async_remote_copy(
            src_ref=src, dst_ref=dst, send_sem=snd.at[index], recv_sem=rcv.at[index],
            device_id=(peer,), device_id_type=MESH,
        )
        if goes is None:
            copy.start()
        else:
            pl.when(goes)(copy.start)
        used.append(Sent(copy, goes, comes))
        return used[-1]

    def shift(src, dst, offset):
        return send(src, dst, at(offset), inside(offset), inside(-offset))

    def relay(src, dst, offset):
        return send(
            src, dst, at(offset), inside(-2 * offset) & inside(offset), inside(-3 * offset)
        )

    def share(piece):
        rows = pl.ds(piece * 256, 256)
        return (
            shift(values.at[rows], nv.at[0, rows], 1),
            shift(values.at[rows], nv.at[1, rows], -1),
        )

    def near(block, points, piece, fresh):
        j = piece * 256

        def step(i, carry):
            row = pl.multiple_of(i * ROWS, ROWS)
            far = None
            for axis in range(3):
                own = pb[axis, pl.ds(row, ROWS), :]
                gap = jnp.concatenate([own, own], axis=1) - points[axis:axis + 1, j:j + 256]
                far = gap * gap if far is None else far + gap * gap
            k_hi, k_lo = split(jnp.exp2(-far))
            both = block[j:j + 256, :]
            term = dot(k_hi, both)
            total = term[:, :NCOL] + term[:, NCOL:] + dot(k_lo, both[:, :NCOL])
            if fresh:
                out[pl.ds(row, ROWS), :] = total
            else:
                out[pl.ds(row, ROWS), :] += total
            return carry

        lax.fori_loop(0, LEAF // ROWS, step, 0)

    def near_side(side, sent, piece):
        def work():
            rows = pl.ds(piece * 256, 256)
            w_hi, w_lo = split(nv[side, rows, :])
            nst[side, rows, :NCOL] = w_hi
            nst[side, rows, NCOL:] = w_lo
            near(nst.at[side], nc.at[side], piece, False)

        sent[side].wait_recv()
        pl.when(inside(-1 if side == 0 else 1))(work)


    def choose(buf, level, slot):
        delta = inter[slot, level] - me // 2 ** level
        return jnp.where(
            delta == -2, buf[0], jnp.where(delta == -3, buf[1], jnp.where(delta == 2, buf[2], buf[3]))
        )

    def coupled(buf, level, first, count):
        both = jnp.concatenate([choose(buf, level, 0), choose(buf, level, 1)], axis=0).T
        rows = pl.ds(first, count)
        return (
            dot3(split(both[:64]), split(cw[0, rows, :]))
            + dot3(split(both[64:]), split(cw[1, rows, :]))
        ) * 2.0 ** (-level / 2.0)

    keep = pl.multiple_of(core * 64, 64)
    give = pl.multiple_of((1 - core) * 64, 64)
    e3_own = e3.at[pl.ds(e3_row, 64)]
    e3_far = send(transfers.at[pl.ds(384, 64)], e3_own, p2)
    e3_near = send(transfers.at[pl.ds(384, 64)], e3_own, p1)
    e2_near = send(transfers.at[pl.ds(256, 128)], e2.at[pl.ds(e2_row, 128)], p1)
    v0 = share(0)

    get_values.wait()
    v_hi, v_lo = split(val[...])
    vst[:, :NCOL] = v_hi
    vst[:, NCOL:] = v_lo
    vt_hi, vt_lo = split(val[...].T)
    c0_t = dot3((vt_hi, vt_lo), (bt_hi[...], bt_lo[...]))
    c0[...] = c0_t
    get_e1.wait()
    t1_t = dot3(split(c0_t), split(e1[...]))
    t1[...] = t1_t
    get_e2.wait()
    get_e3.wait()

    s1 = send(t1.at[pl.ds(give, 64)], t1r, p1)
    s0_up = shift(c0, r0.at[0], 2)
    s0_down = shift(c0, r0.at[2], -2)
    cw_near = send(couplings.at[pl.ds(512, 448)], cw.at[core], p1)
    for axis in range(3):
        pb[axis] = jnp.broadcast_to(pc[:, axis:axis + 1], (LEAF, NCOL))
    near(vst, cs, 0, True)

    s1.wait_recv()
    c1_t = t1[pl.ds(keep, 64), :] + t1r[...]
    c1[...] = c1_t
    e2_near.wait_recv()
    t2_t = dot3(split(c1_t), split(e2[...]))
    t2_q = t2_t.T
    for b in range(2):
        t2[b] = jnp.concatenate([t2_q[b * 128:b * 128 + 64], t2_q[b * 128 + 64:b * 128 + 128]], axis=1)
    u2 = send(t2.at[1 - pair], t2r, p2)
    near(vst, cs, 1, False)
    e3_far.wait_recv()
    other = pl.multiple_of((quarter + 2 - 4 * (quarter // 2)) * 64, 64)
    e3_relay = send(e3.at[pl.ds(other, 64)], e3.at[pl.ds(other, 64)], p1)
    near(vst, cs, 2, False)
    e3_near.wait_recv()
    e3_relay.wait_recv()
    t3_t = dot3(split(t2_t), split(e3[...]))
    t3_q = t3_t.T
    for b in range(4):
        t3[b] = jnp.concatenate([t3_q[b * 64:b * 64 + 32], t3_q[b * 64 + 32:b * 64 + 64]], axis=1)
    u3 = []
    for n, peer in enumerate((p2, p4, p6)):
        u3.append(send(t3.at[peer // 2 % 4], t3r.at[n], peer))

    c_up = shift(cs, nc.at[0], 1)
    c_down = shift(cs, nc.at[1], -1)
    s2_up = shift(c1, r1.at[0], 4)
    s2_down = shift(c1, r1.at[2], -4)
    near(vst, cs, 3, False)
    s0_up.wait_recv()
    f0_up = relay(r0.at[0], r0.at[1], 1)
    s0_down.wait_recv()
    f0_down = relay(r0.at[2], r0.at[3], -1)
    u2.wait_recv()
    c2[...] = t2[pair] + t2r[...]
    for copy in u3:
        copy.wait_recv()
    c3[...] = (t3[chip] + t3r[0]) + (t3r[1] + t3r[2])
    s4 = [
        shift(c3, r3.at[0], 16), shift(c3, r3.at[2], -16),
        shift(c3, r3.at[1], 24), shift(c3, r3.at[3], -24),
    ]

    s3_up = shift(c2, r2.at[0], 8)
    s3_down = shift(c2, r2.at[2], -8)
    c_up.wait_recv()
    c_down.wait_recv()
    for n, mat in enumerate((e1, e2, e3)):
        et[2 * n], et[2 * n + 1] = split(mat[...].T)
    near_side(0, v0, 0)
    near_side(1, v0, 0)
    s2_up.wait_recv()
    f2_up = relay(r1.at[0], r1.at[1], 2)
    s2_down.wait_recv()
    f2_down = relay(r1.at[2], r1.at[3], -2)
    f0_up.wait_recv()
    f0_down.wait_recv()
    both0 = jnp.concatenate([choose(r0, 0, 0), choose(r0, 0, 1)], axis=1)
    get_cp0.wait()
    y0[...] = dot3(split(both0), split(cp0[...]))

    v1 = share(1)
    s3_up.wait_recv()
    f3_up = relay(r2.at[0], r2.at[1], 4)
    s3_down.wait_recv()
    f3_down = relay(r2.at[2], r2.at[3], -4)
    get_cw.wait()
    cw_near.wait_recv()
    for copy in s4:
        copy.wait_recv()
    h3[...] = coupled(r3, 3, 384, 64)
    q3 = []
    for n, peer in enumerate((p2, p4, p6)):
        piece = pl.multiple_of(peer // 2 % 4 * 16, 16)
        q3.append(send(h3.at[pl.ds(piece, 16)], h3r.at[n], peer))

    v2 = share(2)
    near_side(0, v1, 1)
    f3_up.wait_recv()
    f3_down.wait_recv()
    h2[...] = coupled(r2, 2, 256, 128)
    q2 = send(h2, h2r, p2)
    f2_up.wait_recv()
    f2_down.wait_recv()
    both1 = jnp.concatenate([choose(r1, 1, 0), choose(r1, 1, 1)], axis=1)
    rows1 = jnp.concatenate(
        [cw[0, pl.ds(0, 128), :], cw[1, pl.ds(0, 128), :], cw[0, pl.ds(128, 128), :], cw[1, pl.ds(128, 128), :]],
        axis=0,
    )
    y1[...] = dot3(split(both1), split(rows1)) * 2.0 ** -0.5
    for copy in q3:
        copy.wait_recv()
    mine = pl.multiple_of(chip * 16, 16)
    f3[pl.ds(mine, 16), :] = (h3[pl.ds(mine, 16), :] + h3r[0]) + (h3r[1] + h3r[2])
    g3 = []
    for peer in (p2, p4, p6):
        g3.append(send(f3.at[pl.ds(mine, 16)], f3.at[pl.ds(mine, 16)], peer))

    v3 = share(3)
    near_side(1, v1, 1)
    near_side(0, v2, 2)
    near_side(1, v2, 2)
    q2.wait_recv()
    for copy in g3:
        copy.wait_recv()
    f2_t = (h2[...] + h2r[...]) + dot3(split(f3[...]), (et[4], et[5]))
    f1_half = y1[...] + dot3(split(f2_t), (et[2], et[3]))
    f1[pl.ds(keep, 64), :] = f1_half
    g1 = send(f1.at[pl.ds(keep, 64)], f1.at[pl.ds(keep, 64)], p1)
    near_side(0, v3, 3)
    near_side(1, v3, 3)
    g1.wait_recv()
    f0 = y0[...] + dot3(split(f1[...]), (et[0], et[1]))
    f0_hi, f0_lo = split(f0.T)
    f0_both = jnp.concatenate([f0_hi, f0_lo], axis=1)

    def finish(i, carry):
        row = pl.multiple_of(i * ROWS, ROWS)
        first = dot(bt_hi[pl.ds(row, ROWS), :], f0_both)
        second = dot(bt_lo[pl.ds(row, ROWS), :], f0_hi)
        out[pl.ds(row, ROWS), :] += first[:, :NCOL] + (first[:, NCOL:] + second)
        return carry

    lax.fori_loop(0, LEAF // ROWS, finish, 0)
    for copy in used:
        copy.wait_send()


def per_device(values, coords, permutation, basis, transfers, couplings, interactions):
    vmem = pl.BlockSpec(memory_space=pltpu.VMEM)
    smem = pl.BlockSpec(memory_space=pltpu.SMEM)
    hbm = pl.BlockSpec(memory_space=pltpu.HBM)

    def f32(*shape):
        return pltpu.VMEM(shape, F32)

    def b16(*shape):
        return pltpu.VMEM(shape, BF16)

    copies = 64
    return pl.pallas_call(
        kernel,
        out_shape=jax.ShapeDtypeStruct((LEAF, NCOL), F32),
        in_specs=[hbm, hbm, hbm, hbm, hbm, hbm, smem],
        out_specs=vmem,
        scratch_shapes=[
            f32(3, LEAF), pltpu.VMEM((1, LEAF), jnp.int32),
            f32(LEAF, NCOL), f32(LEAF, RANK), f32(256, 256), f32(256, 256), f32(256, 256),
            f32(512, 256), f32(2, 448, 256), f32(8, LEAF), f32(LEAF, 8), f32(3, LEAF, NCOL), b16(LEAF, 256), b16(2, LEAF, 256),
            f32(2, LEAF, NCOL), f32(2, 8, LEAF), b16(LEAF, 512), b16(LEAF, 256), b16(LEAF, 256),
            f32(128, 256), f32(128, 256), f32(64, 256), f32(64, 256),
            f32(2, 64, 128), f32(64, 128), f32(4, 32, 128), f32(3, 32, 128),
            f32(64, 128), f32(32, 128),
            f32(4, 128, 256), f32(4, 64, 256), f32(4, 64, 128), f32(4, 32, 128),
            f32(64, 256), f32(64, 256), f32(64, 256), f32(3, 16, 256), f32(64, 256),
            f32(128, 256), f32(128, 256), f32(64, 256), b16(6, 256, 256),
            pltpu.SemaphoreType.DMA((9,)),
            pltpu.SemaphoreType.DMA((copies,)),
            pltpu.SemaphoreType.DMA((copies,)),
        ],
        compiler_params=pltpu.CompilerParams(
            collective_id=0, has_side_effects=True, vmem_limit_bytes=63 * 2 ** 20
        ),
        cost_estimate=pl.CostEstimate(
            flops=3 * 2 ** 30, bytes_accessed=4 * 2 ** 20, transcendentals=3 * 2 ** 20
        ),
    )(
        values, coords, permutation.reshape(1, LEAF), basis, transfers, couplings,
        interactions.transpose(0, 2, 1).reshape(2, 4),
    )


def solution(mesh):
    in_specs = (
        P("leaf", None),
        P(None, "leaf"),
        P("leaf"),
        P("leaf", None),
        P("leaf", None),
        P("leaf", None),
        P("leaf", None, None),
    )
    out_specs = P("leaf", None)
    return jax.shard_map(
        per_device, mesh=mesh, in_specs=in_specs, out_specs=out_specs, check_vma=False
    )
```

```python
import functools
import math

import jax
import jax.numpy as jnp
from jax import lax
from jax.experimental import pallas as pl
from jax.experimental.pallas import tpu as pltpu
from jax.sharding import PartitionSpec as P

LEAF = 1024
RANK = 256
NCOL = 128
N_LEAF = 512
ROWS = 256
MESH = pl.DeviceIdType.MESH
F32 = jnp.float32
BF16 = jnp.bfloat16
NT = (((1,), (1,)), ((), ()))
NN = (((1,), (0,)), ((), ()))
SCALE = math.sqrt(8.0 * math.log2(math.e))


def split(x):
    hi = x.astype(BF16)
    return hi, (x - hi.astype(F32)).astype(BF16)


def dot(a, b, dims=NN):
    return lax.dot_general(a, b, dims, preferred_element_type=F32)


def dot3(a, b, dims=NN):
    a_hi, a_lo = a
    b_hi, b_lo = b
    return dot(a_hi, b_hi, dims) + (dot(a_hi, b_lo, dims) + dot(a_lo, b_hi, dims))


def kernel(
    values, coords_in, perm_in, basis, transfers, couplings, inter, out,
    coords, perm,
    val, bas, e1, e2, e3, cp0, cw, cs, pc, pb, vst, nst, nv, nc, oh_b, bt_hi, bt_lo,
    c0, t1, t1r, c1, t2, t2r, t3, t3r, c2, c3, r0, r1, r2, r3,
    h2, h2r, h3, h3r, f3, f1, y0, y1, et,
    loc, snd, rcv,
):
    me = lax.axis_index("leaf")
    core = me % 2
    quarter = me % 4
    pair = me // 2 % 2
    chip = me // 2 % 4

    def at(offset):
        return (me + offset + N_LEAF) % N_LEAF

    p1 = me + 1 - 2 * core
    p2 = me + 2 - 4 * (me // 2 % 2)
    p4 = me + 4 - 8 * (me // 4 % 2)
    p6 = p2 + 4 - 8 * (me // 4 % 2)
    p3 = p2 + 1 - 2 * core

    barrier = pltpu.get_barrier_semaphore()

    def inside(offset):
        return (me + offset >= 0) & (me + offset < N_LEAF)

    def greet(peer):
        pl.semaphore_signal(barrier, inc=1, device_id=(peer,), device_id_type=MESH)

    group = (p1, p2, p3, p4, p6)
    for peer in group:
        greet(peer)
    expected = len(group)
    for offset in (1, -1, 2, -2, 4, -4, 8, -8, 16, -16, 24, -24):
        pl.when(inside(offset))(functools.partial(greet, at(offset)))
        expected = expected + jnp.where(inside(offset), 1, 0)

    local = []

    def bring(src, dst):
        copy = pltpu.make_async_copy(src, dst, loc.at[len(local)])
        copy.start()
        local.append(copy)
        return copy

    e2_row = pl.multiple_of(core * 128, 128)
    e3_row = pl.multiple_of(quarter * 64, 64)
    get_coords = bring(coords_in, coords)
    get_perm = bring(perm_in, perm)
    get_basis = bring(basis, bas)
    get_values = bring(values, val)
    get_e1 = bring(transfers.at[pl.ds(0, 256)], e1)
    get_e2 = bring(transfers.at[pl.ds(256, 128)], e2.at[pl.ds(e2_row, 128)])
    get_e3 = bring(transfers.at[pl.ds(384, 64)], e3.at[pl.ds(e3_row, 64)])
    get_cp0 = bring(couplings.at[pl.ds(0, 512)], cp0)
    get_cw = bring(couplings.at[pl.ds(512, 448)], cw.at[core])

    get_coords.wait()
    cs[pl.ds(0, 3), :] = coords[...] * SCALE
    cs[pl.ds(3, 5), :] = jnp.zeros((5, LEAF), F32)
    pc[...] = cs[...].T

    get_basis.wait()
    b_hi, b_lo = split(bas[...])
    oh_b[:, :RANK] = b_hi
    oh_b[:, RANK:] = b_lo
    get_perm.wait()
    order = perm[...] % LEAF

    def place(i, carry):
        row = pl.multiple_of(i * ROWS, ROWS)
        point = lax.broadcasted_iota(jnp.int32, (ROWS, LEAF), 0) + row
        hot = jnp.where(point == order, 1.0, 0.0).astype(BF16)
        moved = dot(hot, oh_b[...])
        bt_hi[pl.ds(row, ROWS), :] = moved[:, :RANK].astype(BF16)
        bt_lo[pl.ds(row, ROWS), :] = moved[:, RANK:].astype(BF16)
        return carry

    lax.fori_loop(0, LEAF // ROWS, place, 0)
    pl.semaphore_wait(barrier, expected)

    used = []

    class Sent:
        def __init__(self, copy, goes, comes):
            self.copy, self.goes, self.comes = copy, goes, comes

        def wait_recv(self):
            if self.comes is None:
                self.copy.wait_recv()
            else:
                pl.when(self.comes)(self.copy.wait_recv)

        def wait_send(self):
            if self.goes is None:
                self.copy.wait_send()
            else:
                pl.when(self.goes)(self.copy.wait_send)

    def send(src, dst, peer, goes=None, comes=None):
        index = len(used)
        copy = pltpu.make_async_remote_copy(
            src_ref=src, dst_ref=dst, send_sem=snd.at[index], recv_sem=rcv.at[index],
            device_id=(peer,), device_id_type=MESH,
        )
        if goes is None:
            copy.start()
        else:
            pl.when(goes)(copy.start)
        used.append(Sent(copy, goes, comes))
        return used[-1]

    def shift(src, dst, offset):
        return send(src, dst, at(offset), inside(offset), inside(-offset))

    def relay(src, dst, offset):
        return send(
            src, dst, at(offset), inside(-2 * offset) & inside(offset), inside(-3 * offset)
        )

    def share(piece):
        rows = pl.ds(piece * 256, 256)
        return (
            shift(values.at[rows], nv.at[0, rows], 1),
            shift(values.at[rows], nv.at[1, rows], -1),
        )

    def near(block, points, piece, fresh):
        j = piece * 256

        def step(i, carry):
            row = pl.multiple_of(i * ROWS, ROWS)
            far = None
            for axis in range(3):
                own = pb[axis, pl.ds(row, ROWS), :]
                gap = jnp.concatenate([own, own], axis=1) - points[axis:axis + 1, j:j + 256]
                far = gap * gap if far is None else far + gap * gap
            k_hi, k_lo = split(jnp.exp2(-far))
            both = block[j:j + 256, :]
            term = dot(k_hi, both)
            total = term[:, :NCOL] + term[:, NCOL:] + dot(k_lo, both[:, :NCOL])
            if fresh:
                out[pl.ds(row, ROWS), :] = total
            else:
                out[pl.ds(row, ROWS), :] += total
            return carry

        lax.fori_loop(0, LEAF // ROWS, step, 0)

    def near_side(side, sent, piece):
        def work():
            rows = pl.ds(piece * 256, 256)
            w_hi, w_lo = split(nv[side, rows, :])
            nst[side, rows, :NCOL] = w_hi
            nst[side, rows, NCOL:] = w_lo
            near(nst.at[side], nc.at[side], piece, False)

        sent[side].wait_recv()
        pl.when(inside(-1 if side == 0 else 1))(work)


    def choose(buf, level, slot):
        delta = inter[slot, level] - me // 2 ** level
        return jnp.where(
            delta == -2, buf[0], jnp.where(delta == -3, buf[1], jnp.where(delta == 2, buf[2], buf[3]))
        )

    def coupled(buf, level, first, count):
        both = jnp.concatenate([choose(buf, level, 0), choose(buf, level, 1)], axis=0).T
        rows = pl.ds(first, count)
        return (
            dot3(split(both[:64]), split(cw[0, rows, :]))
            + dot3(split(both[64:]), split(cw[1, rows, :]))
        ) * 2.0 ** (-level / 2.0)

    keep = pl.multiple_of(core * 64, 64)
    give = pl.multiple_of((1 - core) * 64, 64)
    e3_own = e3.at[pl.ds(e3_row, 64)]
    e3_far = send(transfers.at[pl.ds(384, 64)], e3_own, p2)
    e3_near = send(transfers.at[pl.ds(384, 64)], e3_own, p1)
    e2_near = send(transfers.at[pl.ds(256, 128)], e2.at[pl.ds(e2_row, 128)], p1)
    v0 = share(0)

    get_values.wait()
    v_hi, v_lo = split(val[...])
    vst[:, :NCOL] = v_hi
    vst[:, NCOL:] = v_lo
    vt_hi, vt_lo = split(val[...].T)
    c0_t = dot3((vt_hi, vt_lo), (bt_hi[...], bt_lo[...]))
    c0[...] = c0_t
    get_e1.wait()
    t1_t = dot3(split(c0_t), split(e1[...]))
    t1[...] = t1_t
    get_e2.wait()
    get_e3.wait()

    s1 = send(t1.at[pl.ds(give, 64)], t1r, p1)
    s0_up = shift(c0, r0.at[0], 2)
    s0_down = shift(c0, r0.at[2], -2)
    cw_near = send(couplings.at[pl.ds(512, 448)], cw.at[core], p1)
    for axis in range(3):
        pb[axis] = jnp.broadcast_to(pc[:, axis:axis + 1], (LEAF, NCOL))
    near(vst, cs, 0, True)

    s1.wait_recv()
    c1_t = t1[pl.ds(keep, 64), :] + t1r[...]
    c1[...] = c1_t
    e2_near.wait_recv()
    t2_t = dot3(split(c1_t), split(e2[...]))
    t2_q = t2_t.T
    for b in range(2):
        t2[b] = jnp.concatenate([t2_q[b * 128:b * 128 + 64], t2_q[b * 128 + 64:b * 128 + 128]], axis=1)
    u2 = send(t2.at[1 - pair], t2r, p2)
    near(vst, cs, 1, False)
    e3_far.wait_recv()
    other = pl.multiple_of((quarter + 2 - 4 * (quarter // 2)) * 64, 64)
    e3_relay = send(e3.at[pl.ds(other, 64)], e3.at[pl.ds(other, 64)], p1)
    near(vst, cs, 2, False)
    e3_near.wait_recv()
    e3_relay.wait_recv()
    t3_t = dot3(split(t2_t), split(e3[...]))
    t3_q = t3_t.T
    for b in range(4):
        t3[b] = jnp.concatenate([t3_q[b * 64:b * 64 + 32], t3_q[b * 64 + 32:b * 64 + 64]], axis=1)
    u3 = []
    for n, peer in enumerate((p2, p4, p6)):
        u3.append(send(t3.at[peer // 2 % 4], t3r.at[n], peer))

    c_up = shift(cs, nc.at[0], 1)
    c_down = shift(cs, nc.at[1], -1)
    s2_up = shift(c1, r1.at[0], 4)
    s2_down = shift(c1, r1.at[2], -4)
    near(vst, cs, 3, False)
    s0_up.wait_recv()
    f0_up = relay(r0.at[0], r0.at[1], 1)
    s0_down.wait_recv()
    f0_down = relay(r0.at[2], r0.at[3], -1)
    u2.wait_recv()
    c2[...] = t2[pair] + t2r[...]
    for copy in u3:
        copy.wait_recv()
    c3[...] = (t3[chip] + t3r[0]) + (t3r[1] + t3r[2])
    s4 = [
        shift(c3, r3.at[0], 16), shift(c3, r3.at[2], -16),
        shift(c3, r3.at[1], 24), shift(c3, r3.at[3], -24),
    ]

    s3_up = shift(c2, r2.at[0], 8)
    s3_down = shift(c2, r2.at[2], -8)
    c_up.wait_recv()
    c_down.wait_recv()
    for n, mat in enumerate((e1, e2, e3)):
        et[2 * n], et[2 * n + 1] = split(mat[...].T)
    near_side(0, v0, 0)
    near_side(1, v0, 0)
    s2_up.wait_recv()
    f2_up = relay(r1.at[0], r1.at[1], 2)
    s2_down.wait_recv()
    f2_down = relay(r1.at[2], r1.at[3], -2)
    f0_up.wait_recv()
    f0_down.wait_recv()
    both0 = jnp.concatenate([choose(r0, 0, 0), choose(r0, 0, 1)], axis=1)
    get_cp0.wait()
    y0[...] = dot3(split(both0), split(cp0[...]))

    s3_up.wait_recv()
    f3_up = relay(r2.at[0], r2.at[1], 4)
    s3_down.wait_recv()
    f3_down = relay(r2.at[2], r2.at[3], -4)
    v1 = share(1)
    get_cw.wait()
    cw_near.wait_recv()
    for copy in s4:
        copy.wait_recv()
    h3[...] = coupled(r3, 3, 384, 64)
    q3 = []
    for n, peer in enumerate((p2, p4, p6)):
        piece = pl.multiple_of(peer // 2 % 4 * 16, 16)
        q3.append(send(h3.at[pl.ds(piece, 16)], h3r.at[n], peer))

    v2 = share(2)
    near_side(0, v1, 1)
    f3_up.wait_recv()
    f3_down.wait_recv()
    h2[...] = coupled(r2, 2, 256, 128)
    q2 = send(h2, h2r, p2)
    f2_up.wait_recv()
    f2_down.wait_recv()
    both1 = jnp.concatenate([choose(r1, 1, 0), choose(r1, 1, 1)], axis=1)
    rows1 = jnp.concatenate(
        [cw[0, pl.ds(0, 128), :], cw[1, pl.ds(0, 128), :], cw[0, pl.ds(128, 128), :], cw[1, pl.ds(128, 128), :]],
        axis=0,
    )
    y1[...] = dot3(split(both1), split(rows1)) * 2.0 ** -0.5
    for copy in q3:
        copy.wait_recv()
    mine = pl.multiple_of(chip * 16, 16)
    f3[pl.ds(mine, 16), :] = (h3[pl.ds(mine, 16), :] + h3r[0]) + (h3r[1] + h3r[2])
    g3 = []
    for peer in (p2, p4, p6):
        g3.append(send(f3.at[pl.ds(mine, 16)], f3.at[pl.ds(mine, 16)], peer))

    v3 = share(3)
    near_side(1, v1, 1)
    near_side(0, v2, 2)
    near_side(1, v2, 2)
    q2.wait_recv()
    for copy in g3:
        copy.wait_recv()
    f2_t = (h2[...] + h2r[...]) + dot3(split(f3[...]), (et[4], et[5]))
    f1_half = y1[...] + dot3(split(f2_t), (et[2], et[3]))
    f1[pl.ds(keep, 64), :] = f1_half
    g1 = send(f1.at[pl.ds(keep, 64)], f1.at[pl.ds(keep, 64)], p1)
    near_side(0, v3, 3)
    near_side(1, v3, 3)
    g1.wait_recv()
    f0 = y0[...] + dot3(split(f1[...]), (et[0], et[1]))
    f0_hi, f0_lo = split(f0.T)
    f0_both = jnp.concatenate([f0_hi, f0_lo], axis=1)

    def finish(i, carry):
        row = pl.multiple_of(i * ROWS, ROWS)
        first = dot(bt_hi[pl.ds(row, ROWS), :], f0_both)
        second = dot(bt_lo[pl.ds(row, ROWS), :], f0_hi)
        out[pl.ds(row, ROWS), :] += first[:, :NCOL] + (first[:, NCOL:] + second)
        return carry

    lax.fori_loop(0, LEAF // ROWS, finish, 0)
    for copy in used:
        copy.wait_send()


def per_device(values, coords, permutation, basis, transfers, couplings, interactions):
    vmem = pl.BlockSpec(memory_space=pltpu.VMEM)
    smem = pl.BlockSpec(memory_space=pltpu.SMEM)
    hbm = pl.BlockSpec(memory_space=pltpu.HBM)

    def f32(*shape):
        return pltpu.VMEM(shape, F32)

    def b16(*shape):
        return pltpu.VMEM(shape, BF16)

    copies = 64
    return pl.pallas_call(
        kernel,
        out_shape=jax.ShapeDtypeStruct((LEAF, NCOL), F32),
        in_specs=[hbm, hbm, hbm, hbm, hbm, hbm, smem],
        out_specs=vmem,
        scratch_shapes=[
            f32(3, LEAF), pltpu.VMEM((1, LEAF), jnp.int32),
            f32(LEAF, NCOL), f32(LEAF, RANK), f32(256, 256), f32(256, 256), f32(256, 256),
            f32(512, 256), f32(2, 448, 256), f32(8, LEAF), f32(LEAF, 8), f32(3, LEAF, NCOL), b16(LEAF, 256), b16(2, LEAF, 256),
            f32(2, LEAF, NCOL), f32(2, 8, LEAF), b16(LEAF, 512), b16(LEAF, 256), b16(LEAF, 256),
            f32(128, 256), f32(128, 256), f32(64, 256), f32(64, 256),
            f32(2, 64, 128), f32(64, 128), f32(4, 32, 128), f32(3, 32, 128),
            f32(64, 128), f32(32, 128),
            f32(4, 128, 256), f32(4, 64, 256), f32(4, 64, 128), f32(4, 32, 128),
            f32(64, 256), f32(64, 256), f32(64, 256), f32(3, 16, 256), f32(64, 256),
            f32(128, 256), f32(128, 256), f32(64, 256), b16(6, 256, 256),
            pltpu.SemaphoreType.DMA((9,)),
            pltpu.SemaphoreType.DMA((copies,)),
            pltpu.SemaphoreType.DMA((copies,)),
        ],
        compiler_params=pltpu.CompilerParams(
            collective_id=0, has_side_effects=True, vmem_limit_bytes=63 * 2 ** 20
        ),
        cost_estimate=pl.CostEstimate(
            flops=3 * 2 ** 30, bytes_accessed=4 * 2 ** 20, transcendentals=3 * 2 ** 20
        ),
    )(
        values, coords, permutation.reshape(1, LEAF), basis, transfers, couplings,
        interactions.transpose(0, 2, 1).reshape(2, 4),
    )


def solution(mesh):
    in_specs = (
        P("leaf", None),
        P(None, "leaf"),
        P("leaf"),
        P("leaf", None),
        P("leaf", None),
        P("leaf", None),
        P("leaf", None, None),
    )
    out_specs = P("leaf", None)
    return jax.shard_map(
        per_device, mesh=mesh, in_specs=in_specs, out_specs=out_specs, check_vma=False
    )
```
